128 devices in a mesh: gx: 8 (over y_lo, z), gy: 16 (over y_hi, x, core).
Axes of the slice: x: 4, y: 4 (y_hi: 2, y_lo: 2; y = y_hi * 2 + y_lo), z: 4, core: 2. Of those that a mesh axis runs over, the one named last changes fastest.
Arguments:
- tokens: bfloat16 [2048, 6144], P('gy', 'gx'), may hold values from -6 to 6
- up_weight: bfloat16 [6144, 24576], P('gx', 'gy'), may hold values from -0.078125 to 0.078125
- down_weight: bfloat16 [24576, 6144], P('gy', 'gx'), may hold values from -0.078125 to 0.078125
- out_grad: bfloat16 [2048, 6144], P('gy', 'gx'), may hold values from -6 to 6
Outputs:
- input_grad: bfloat16 [2048, 6144], P('gy', 'gx')
- up_grad: bfloat16 [6144, 24576], P('gx', 'gy')
- down_grad: bfloat16 [24576, 6144], P('gy', 'gx')
The draws below stay inside these ranges and needn't reach their ends.
All inputs are finite; a program needn't handle non-finite values.
Results may differ from the reference program's by a relative error of at most 0.027.
Values may be sent and summed in bfloat16 or wider, within the bound.
No kernel may reach another device: no remote copies, remote signals or barrier semaphores. Data moves between devices by JAX's collectives and lax.ppermute only.
A program may use at most 128 MiB of HBM per device.

```python
import math
import jax
import jax.numpy as jnp

D = 6144
FF = 24576
TOKENS = 2048
N_GX = 8


def block_scale(stream_key, dims, split, smallest, high):
    level = 1.0
    for dim, shards_of in split:
        steps = jax.random.uniform(jax.random.fold_in(jax.random.fold_in(stream_key, 6), dim), (shards_of,), jnp.float32, smallest / len(split), high / len(split))
        level = level * jnp.repeat(jnp.exp(steps), dims[dim] // shards_of).reshape((-1,) + (1,) * (len(dims) - 1 - dim))
    return level


def scatter_about(own_key, dims, scale, reach, split=(), held_as=jnp.bfloat16):
    result = scale * jax.random.normal(own_key, dims, jnp.float32)
    if split:
        result = result * block_scale(own_key, dims, split, -0.22, 0.18)
    return jnp.clip(result, -reach, reach).astype(held_as)


def setup_inputs(seed: int = 0) -> dict:
    key_list = jax.random.split(jax.random.key(seed), 5)
    return {
        "tokens": scatter_about(key_list[0], (TOKENS, D), 1.0, 6.0, ((0, 16), (1, 8))),
        "up_weight": scatter_about(key_list[1], (D, FF), D ** -0.5, 0.078125, ((0, 8), (1, 16))),
        "down_weight": scatter_about(key_list[2], (FF, D), D ** -0.5, 0.078125, ((0, 16), (1, 8))),
        "out_grad": scatter_about(key_list[3], (TOKENS, D), 1.0, 6.0, ((0, 16), (1, 8))),
    }


def reference(tokens, up_weight, down_weight, out_grad):
    width = D // N_GX
    pre = jnp.zeros((TOKENS, FF), jnp.float32)
    act_grad = jnp.zeros((TOKENS, FF), jnp.float32)
    for block in range(N_GX):
        lo = block * width
        hi = lo + width
        part = jnp.dot(tokens[:, lo:hi], up_weight[lo:hi, :], preferred_element_type=jnp.float32)
        pre = pre + part.astype(jnp.bfloat16).astype(jnp.float32)
        back = jnp.dot(out_grad[:, lo:hi], down_weight[:, lo:hi].T, preferred_element_type=jnp.float32)
        act_grad = act_grad + back.astype(jnp.bfloat16).astype(jnp.float32)
    cdf = 0.5 * (1.0 + jax.scipy.special.erf(pre / math.sqrt(2.0)))
    act = (pre * cdf).astype(jnp.bfloat16)
    slope = cdf + pre * jnp.exp(-0.5 * pre * pre) / math.sqrt(2.0 * math.pi)
    pre_grad = (act_grad * slope).astype(jnp.bfloat16)
    input_grad = jnp.dot(pre_grad, up_weight.T, preferred_element_type=jnp.float32).astype(jnp.bfloat16)
    factor = 1.0 / math.sqrt(TOKENS)
    up_grad = (jnp.dot(tokens.T, pre_grad, preferred_element_type=jnp.float32) * factor).astype(jnp.bfloat16)
    down_grad = (jnp.dot(act.T, out_grad, preferred_element_type=jnp.float32) * factor).astype(jnp.bfloat16)
    return (input_grad, up_grad, down_grad)
```

```python
import math

import jax
import jax.numpy as jnp
from jax import lax
from jax.sharding import PartitionSpec as P

Z = 4
X = 4
BF16, F32 = jnp.bfloat16, jnp.float32


def swap_y(a):
    return lax.ppermute(a, "gx", [(i, (i + Z) % (2 * Z)) for i in range(2 * Z)])


def swap_core(a):
    return lax.ppermute(a, "gy", [(i, i ^ 1) for i in range(4 * X)])


def to_z(a, step):
    return lax.ppermute(a, "gx", [(y * Z + z, y * Z + (z + step) % Z) for y in range(2) for z in range(Z)])


def slot_pairs(slot):
    pairs = []
    for y in range(2):
        for z in range(Z):
            for h in range(2):
                for x in range(X):
                    for c in range(2):
                        user = ((y * Z + z) * 2 + h) * X * 2 + x * 2 + c
                        owner = ((y * Z + z) * 2 + (h ^ c)) * X * 2 + (x + z + slot) % X * 2 + c
                        pairs.append((owner, user))
    return pairs


def fetch(a, slot):
    return lax.ppermute(a, ("gx", "gy"), slot_pairs(slot))


def give_back(a, slot):
    return lax.ppermute(a, ("gx", "gy"), [(user, owner) for owner, user in slot_pairs(slot)])


def add(*terms):
    total = terms[0].astype(F32)
    for t in terms[1:]:
        total = total + t.astype(F32)
    return total


def gather(own):
    wide = jnp.concatenate([own, swap_y(own)], axis=1)
    chip = jnp.concatenate([wide, swap_core(wide)])
    quarters = []
    for slot in range(Z):
        part = fetch(chip, slot)
        quarters.append(jnp.concatenate([part, swap_core(part)]))
    return quarters


def local_step(pre, act_grad):
    cdf = 0.5 * (1.0 + jax.scipy.special.erf(pre / math.sqrt(2.0)))
    act = (pre * cdf).astype(BF16)
    slope = cdf + pre * jnp.exp(-0.5 * pre * pre) / math.sqrt(2.0 * math.pi)
    pre_grad = (act_grad * slope).astype(BF16)
    return (pre_grad, act)


def reduce_z(parts):
    return add(parts[0], *[to_z(parts[r], r) for r in (2, 1, 3)])


def gather_z(own):
    got = {(-r) % Z: to_z(own, r) for r in (2, 1, 3)}
    got[0] = own
    return [got[r] for r in range(Z)]


def dot(a, b, da, db):
    return lax.dot_general(a, b, (((da,), (db,)), ((), ())), preferred_element_type=F32)


def shards(tokens, up_weight, down_weight, out_grad):
    y = lax.axis_index("gx") // Z
    rows, width = tokens.shape
    half = up_weight.shape[1] // 2

    def mine(w, axis):
        return lax.dynamic_slice_in_dim(w, y * half, half, axis=axis)

    def other(w, axis):
        return lax.dynamic_slice_in_dim(w, (1 - y) * half, half, axis=axis)

    def whole(own, got, axis):
        return jnp.where(y == 0, jnp.concatenate([own, got], axis=axis), jnp.concatenate([got, own], axis=axis))

    g = gather(out_grad)
    down = jnp.concatenate([mine(down_weight, 0), swap_y(other(down_weight, 0))], axis=1)
    x = gather(tokens)
    up = jnp.concatenate([mine(up_weight, 1), swap_y(other(up_weight, 1))], axis=0)

    act_grad = reduce_z([dot(q, down, 1, 1).astype(BF16) for q in g])
    pre = reduce_z([dot(q, up, 1, 0).astype(BF16) for q in x])
    pre_grad, act = local_step(pre, act_grad)
    pre_grad, act = gather_z(pre_grad), gather_z(act)

    back = []
    block = 2 * rows
    for slot in range(Z):
        part = dot(pre_grad[slot], up, 1, 1).astype(BF16)
        part = add(part[:block], swap_core(part[block:])).astype(BF16)
        back.append(give_back(part, slot))
    back = add(*back).astype(BF16)
    back = add(back[:rows], swap_core(back[rows:])).astype(BF16)
    input_grad = add(back[:, :width], swap_y(back[:, width:])).astype(BF16)

    factor = 1.0 / math.sqrt(rows * lax.axis_size("gy"))
    up_grad = sum(dot(x[r], pre_grad[r], 0, 0) for r in range(Z))
    up_grad = (up_grad * factor).astype(BF16)
    down_grad = sum(dot(act[r], g[r], 0, 0) for r in range(Z))
    down_grad = (down_grad * factor).astype(BF16)
    up_grad = whole(up_grad[:width], swap_y(up_grad[width:]), 1)
    down_grad = whole(down_grad[:, :width], swap_y(down_grad[:, width:]), 0)
    return (input_grad, up_grad, down_grad)


def solution(mesh):
    in_specs = (P("gy", "gx"), P("gx", "gy"), P("gy", "gx"), P("gy", "gx"))
    out_specs = (P("gy", "gx"), P("gx", "gy"), P("gy", "gx"))
    return jax.shard_map(shards, mesh=mesh, in_specs=in_specs, out_specs=out_specs, check_vma=False)
```

```python
import math

import jax
import jax.numpy as jnp
from jax import lax
from jax.sharding import PartitionSpec as P

Z = 4
X = 4
NEAR, FAR = (1, 3), (0, 2)
BF16, F32 = jnp.bfloat16, jnp.float32


def swap_y(a):
    return lax.ppermute(a, "gx", [(i, (i + Z) % (2 * Z)) for i in range(2 * Z)])


def swap_core(a):
    return lax.ppermute(a, "gy", [(i, i ^ 1) for i in range(4 * X)])


def to_z(a, step):
    return lax.ppermute(a, "gx", [(y * Z + z, y * Z + (z + step) % Z) for y in range(2) for z in range(Z)])


def swap_y_hi(a, flip_lo):
    pairs = []
    for gx in range(2 * Z):
        for gy in range(4 * X):
            other = (gx + Z) % (2 * Z) if flip_lo else gx
            pairs.append((gx * 4 * X + gy, other * 4 * X + (gy + 2 * X) % (4 * X)))
    return lax.ppermute(a, ("gx", "gy"), pairs)


def slot_pairs(slot):
    pairs = []
    for gx in range(2 * Z):
        for h in range(2):
            for x in range(X):
                for c in range(2):
                    first = gx * 4 * X + h * 2 * X + c
                    pairs.append((first + (x + gx + slot) % X * 2, first + x * 2))
    return pairs


def fetch(a, slot):
    return lax.ppermute(a, ("gx", "gy"), slot_pairs(slot))


def give_back(a, slot):
    return lax.ppermute(a, ("gx", "gy"), [(user, owner) for owner, user in slot_pairs(slot)])


def together(*arrays):
    return lax.optimization_barrier(arrays)


def add(*terms):
    total = terms[0].astype(F32)
    for t in terms[1:]:
        total = total + t.astype(F32)
    return total


def along_y(own):
    near, far, across = swap_y(own), swap_y_hi(own, False), swap_y_hi(own, True)
    here = jnp.concatenate([own, near], axis=1)
    there = jnp.concatenate([far, across], axis=1)
    return jnp.concatenate([here, there])


def fetch_pair(chip, pair):
    return [fetch(chip, slot) for slot in pair]


def both_cores(got):
    own = jnp.concatenate(got)
    return jnp.concatenate([own, swap_core(own)])


def quarters(product):
    n = product.shape[0] // 4
    return [jnp.concatenate([product[i * n:(i + 1) * n], product[(i + 2) * n:(i + 3) * n]]) for i in range(2)]


def as_pair(a, b):
    n = a.shape[0] // 2
    return jnp.concatenate([a[:n], b[:n], a[n:], b[n:]])


def local_step(pre, act_grad):
    cdf = 0.5 * (1.0 + jax.scipy.special.erf(pre / math.sqrt(2.0)))
    act = (pre * cdf).astype(BF16)
    slope = cdf + pre * jnp.exp(-0.5 * pre * pre) / math.sqrt(2.0 * math.pi)
    pre_grad = (act_grad * slope).astype(BF16)
    return (pre_grad, act)


def gather_z(own):
    half = own.shape[0] // 2
    behind, ahead = to_z(own, 1), to_z(own, -1)
    return behind, ahead, half


def finish_z(own, near):
    behind, ahead, half = near
    far = jnp.concatenate([to_z(behind[:half], 1), to_z(ahead[half:], -1)])
    return [own, ahead, far, behind]


def dot(a, b, da, db):
    return lax.dot_general(a, b, (((da,), (db,)), ((), ())), preferred_element_type=F32)


def shards(tokens, up_weight, down_weight, out_grad):
    y = lax.axis_index("gx") // Z
    rows, width = tokens.shape
    half = up_weight.shape[1] // 2

    def mine(w, axis):
        return lax.dynamic_slice_in_dim(w, y * half, half, axis=axis)

    def other(w, axis):
        return lax.dynamic_slice_in_dim(w, (1 - y) * half, half, axis=axis)

    def whole(own, got, axis):
        return jnp.where(y == 0, jnp.concatenate([own, got], axis=axis), jnp.concatenate([got, own], axis=axis))

    g_chip = along_y(out_grad)
    down_got = swap_y(other(down_weight, 0))
    near_g = fetch_pair(g_chip, NEAR)
    g_chip, near_g, tokens, down_got = together(g_chip, near_g, tokens, down_got)
    far_g = fetch_pair(g_chip, FAR)
    x_chip = along_y(tokens)
    near_g = both_cores(near_g)
    x_chip, up_other = together(x_chip, other(up_weight, 1))
    up_got = swap_y(up_other)
    down = jnp.concatenate([mine(down_weight, 0), down_got], axis=1)
    one, three = quarters(dot(near_g, down, 1, 1).astype(BF16))
    x_chip, far_g, one, three = together(x_chip, far_g, one, three)
    one, three = to_z(one, 1), to_z(three, 3)
    far_g = both_cores(far_g)
    own, two = quarters(dot(far_g, down, 1, 1).astype(BF16))
    x_chip, two = together(x_chip, two)
    near_x = fetch_pair(x_chip, NEAR)
    x_chip, up_got, near_x, one, three = together(x_chip, up_got, near_x, one, three)
    far_x = fetch_pair(x_chip, FAR)
    act_grad = [own, one, three]
    two = to_z(two, 2)
    up = jnp.concatenate([mine(up_weight, 1), up_got], axis=0)

    near_x = both_cores(near_x)
    one, three = quarters(dot(near_x, up, 1, 0).astype(BF16))
    far_x, two, one, three = together(far_x, two, one, three)
    one, three = to_z(one, 1), to_z(three, 3)
    act_grad.append(two)
    far_x = both_cores(far_x)
    own, two = quarters(dot(far_x, up, 1, 0).astype(BF16))
    pre = [own, one, three, to_z(two, 2)]
    pre_grad, act = local_step(add(*pre), add(*act_grad))

    def rows_back(part):
        part = dot(part, up, 1, 1).astype(BF16)
        n = part.shape[0] // 2
        return part[:n], part[n:]

    def send_back(part, others):
        return add(part, swap_core(others)).astype(BF16)

    own_back = send_back(*rows_back(pre_grad))
    behind, ahead, half = gather_z(pre_grad)
    rows_one, rows_three = rows_back(ahead), rows_back(behind)
    act, own_back, rows_one, rows_three = together(act, own_back, rows_one, rows_three)
    pre_grad = finish_z(pre_grad, (behind, ahead, half))
    act = finish_z(act, gather_z(act))
    back = [give_back(own_back, 0), give_back(send_back(*rows_one), 1), give_back(send_back(*rows_three), 3)]
    back.append(give_back(send_back(*rows_back(pre_grad[2])), 2))
    back = add(*back).astype(BF16)

    up_grad = dot(near_x, as_pair(pre_grad[1], pre_grad[3]), 0, 0)
    up_grad = up_grad + dot(far_x, as_pair(pre_grad[0], pre_grad[2]), 0, 0)
    down_grad = dot(as_pair(act[1], act[3]), near_g, 0, 0)
    down_grad = down_grad + dot(as_pair(act[0], act[2]), far_g, 0, 0)

    here, there = back[:rows], back[rows:]
    far, across = swap_y_hi(there[:, :width], False), swap_y_hi(there[:, width:], True)
    input_grad = add(here[:, :width], swap_y(here[:, width:]), far, across).astype(BF16)

    factor = 1.0 / math.sqrt(rows * lax.axis_size("gy"))
    up_grad = (up_grad * factor).astype(BF16)
    down_grad = (down_grad * factor).astype(BF16)
    up_grad = whole(up_grad[:width], swap_y(up_grad[width:]), 1)
    down_grad = whole(down_grad[:, :width], swap_y(down_grad[:, width:]), 0)
    return (input_grad, up_grad, down_grad)


def solution(mesh):
    in_specs = (P("gy", "gx"), P("gx", "gy"), P("gy", "gx"), P("gy", "gx"))
    out_specs = (P("gy", "gx"), P("gx", "gy"), P("gy", "gx"))
    return jax.shard_map(shards, mesh=mesh, in_specs=in_specs, out_specs=out_specs, check_vma=False)
```

```python
import math

import jax
import jax.numpy as jnp
from jax import lax
from jax.sharding import PartitionSpec as P

Z = 4
X = 4
NEAR, FAR = (1, 3), (0, 2)
BF16, F32 = jnp.bfloat16, jnp.float32


def swap_y(a):
    return lax.ppermute(a, "gx", [(i, (i + Z) % (2 * Z)) for i in range(2 * Z)])


def swap_core(a):
    return lax.ppermute(a, "gy", [(i, i ^ 1) for i in range(4 * X)])


def to_z(a, step):
    return lax.ppermute(a, "gx", [(y * Z + z, y * Z + (z + step) % Z) for y in range(2) for z in range(Z)])


def swap_y_hi(a, flip_lo):
    pairs = []
    for gx in range(2 * Z):
        for gy in range(4 * X):
            other = (gx + Z) % (2 * Z) if flip_lo else gx
            pairs.append((gx * 4 * X + gy, other * 4 * X + (gy + 2 * X) % (4 * X)))
    return lax.ppermute(a, ("gx", "gy"), pairs)


def slot_pairs(slot):
    pairs = []
    for gx in range(2 * Z):
        for h in range(2):
            for x in range(X):
                for c in range(2):
                    first = gx * 4 * X + h * 2 * X + c
                    pairs.append((first + (x + gx + slot) % X * 2, first + x * 2))
    return pairs


def fetch(a, slot):
    return lax.ppermute(a, ("gx", "gy"), slot_pairs(slot))


def give_back(a, slot):
    return lax.ppermute(a, ("gx", "gy"), [(user, owner) for owner, user in slot_pairs(slot)])


def together(*arrays):
    return lax.optimization_barrier(arrays)


def add(*terms):
    total = terms[0].astype(F32)
    for t in terms[1:]:
        total = total + t.astype(F32)
    return total


def along_y(own):
    near, far, across = swap_y(own), swap_y_hi(own, False), swap_y_hi(own, True)
    here = jnp.concatenate([own, near], axis=1)
    there = jnp.concatenate([far, across], axis=1)
    return jnp.concatenate([here, there])


def fetch_pair(chip, pair):
    return [fetch(chip, slot) for slot in pair]


def both_cores(got):
    own = jnp.concatenate(got)
    return jnp.concatenate([own, swap_core(own)])


def quarters(product):
    n = product.shape[0] // 4
    return [jnp.concatenate([product[i * n:(i + 1) * n], product[(i + 2) * n:(i + 3) * n]]) for i in range(2)]


def as_pair(a, b):
    n = a.shape[0] // 2
    return jnp.concatenate([a[:n], b[:n], a[n:], b[n:]])


def local_step(pre, act_grad):
    cdf = 0.5 * (1.0 + jax.scipy.special.erf(pre / math.sqrt(2.0)))
    act = (pre * cdf).astype(BF16)
    slope = cdf + pre * jnp.exp(-0.5 * pre * pre) / math.sqrt(2.0 * math.pi)
    pre_grad = (act_grad * slope).astype(BF16)
    return (pre_grad, act)


def gather_z(own):
    half = own.shape[0] // 2
    behind, ahead = to_z(own, 1), to_z(own, -1)
    return behind, ahead, half


def finish_z(own, near):
    behind, ahead, half = near
    far = jnp.concatenate([to_z(behind[:half], 1), to_z(ahead[half:], -1)])
    return [own, ahead, far, behind]


def dot(a, b, da, db):
    return lax.dot_general(a, b, (((da,), (db,)), ((), ())), preferred_element_type=F32)


def shards(tokens, up_weight, down_weight, out_grad):
    y = lax.axis_index("gx") // Z
    rows, width = tokens.shape
    half = up_weight.shape[1] // 2

    def mine(w, axis):
        return lax.dynamic_slice_in_dim(w, y * half, half, axis=axis)

    def other(w, axis):
        return lax.dynamic_slice_in_dim(w, (1 - y) * half, half, axis=axis)

    def whole(own, got, axis):
        return jnp.where(y == 0, jnp.concatenate([own, got], axis=axis), jnp.concatenate([got, own], axis=axis))

    g_chip = along_y(out_grad)
    x_wide = jnp.concatenate([tokens, swap_y(tokens)], axis=1)
    down_got = swap_y(other(down_weight, 0))
    near_g = fetch_pair(g_chip, NEAR)
    g_chip, near_g, x_wide, down_got = together(g_chip, near_g, x_wide, down_got)
    far_g = fetch_pair(g_chip, FAR)
    x_chip = jnp.concatenate([x_wide, swap_y_hi(x_wide, False)])
    near_g = both_cores(near_g)
    x_chip, up_other = together(x_chip, other(up_weight, 1))
    up_got = swap_y(up_other)
    down = jnp.concatenate([mine(down_weight, 0), down_got], axis=1)
    one, three = quarters(dot(near_g, down, 1, 1).astype(BF16))
    x_chip, far_g, one, three = together(x_chip, far_g, one, three)
    one, three = to_z(one, 1), to_z(three, 3)
    far_g = both_cores(far_g)
    own, two = quarters(dot(far_g, down, 1, 1).astype(BF16))
    near_x = fetch_pair(x_chip, NEAR)
    x_chip, up_got, near_x, one, three, two = together(x_chip, up_got, near_x, one, three, two)
    far_x = fetch_pair(x_chip, FAR)
    act_grad = [own, one, three]
    two = to_z(two, 2)
    up = jnp.concatenate([mine(up_weight, 1), up_got], axis=0)

    near_x = both_cores(near_x)
    one, three = quarters(dot(near_x, up, 1, 0).astype(BF16))
    far_x, two, one, three = together(far_x, two, one, three)
    one, three = to_z(one, 1), to_z(three, 3)
    act_grad.append(two)
    far_x = both_cores(far_x)
    own, two = quarters(dot(far_x, up, 1, 0).astype(BF16))
    pre = [own, one, three, to_z(two, 2)]
    pre_grad, act = local_step(add(*pre), add(*act_grad))

    def rows_back(part):
        part = dot(part, up, 1, 1).astype(BF16)
        n = part.shape[0] // 2
        return part[:n], part[n:]

    def send_back(part, others):
        return add(part, swap_core(others)).astype(BF16)

    own_back = send_back(*rows_back(pre_grad))
    behind, ahead, half = gather_z(pre_grad)
    rows_one, rows_three = rows_back(ahead), rows_back(behind)
    act, own_back, rows_one, rows_three = together(act, own_back, rows_one, rows_three)
    pre_grad = finish_z(pre_grad, (behind, ahead, half))
    act = finish_z(act, gather_z(act))
    back = [give_back(own_back, 0), give_back(send_back(*rows_one), 1), give_back(send_back(*rows_three), 3)]
    back.append(give_back(send_back(*rows_back(pre_grad[2])), 2))
    back = add(*back).astype(BF16)

    up_grad = dot(near_x, as_pair(pre_grad[1], pre_grad[3]), 0, 0)
    up_grad = up_grad + dot(far_x, as_pair(pre_grad[0], pre_grad[2]), 0, 0)
    down_grad = dot(as_pair(act[1], act[3]), near_g, 0, 0)
    down_grad = down_grad + dot(as_pair(act[0], act[2]), far_g, 0, 0)

    here, there = back[:rows], back[rows:]
    far, across = swap_y_hi(there[:, :width], False), swap_y_hi(there[:, width:], True)
    input_grad = add(here[:, :width], swap_y(here[:, width:]), far, across).astype(BF16)

    factor = 1.0 / math.sqrt(rows * lax.axis_size("gy"))
    up_grad = (up_grad * factor).astype(BF16)
    down_grad = (down_grad * factor).astype(BF16)
    up_grad = whole(up_grad[:width], swap_y(up_grad[width:]), 1)
    down_grad = whole(down_grad[:, :width], swap_y(down_grad[:, width:]), 0)
    return (input_grad, up_grad, down_grad)


def solution(mesh):
    in_specs = (P("gy", "gx"), P("gx", "gy"), P("gy", "gx"), P("gy", "gx"))
    out_specs = (P("gy", "gx"), P("gx", "gy"), P("gy", "gx"))
    return jax.shard_map(shards, mesh=mesh, in_specs=in_specs, out_specs=out_specs, check_vma=False)
```

```python
import math

import jax
import jax.numpy as jnp
from jax import lax
from jax.sharding import PartitionSpec as P

Z = 4
X = 4
NEAR, FAR = (1, 3), (0, 2)
BF16, F32 = jnp.bfloat16, jnp.float32


def swap_y(a):
    return lax.ppermute(a, "gx", [(i, (i + Z) % (2 * Z)) for i in range(2 * Z)])


def swap_core(a):
    return lax.ppermute(a, "gy", [(i, i ^ 1) for i in range(4 * X)])


def to_z(a, step):
    return lax.ppermute(a, "gx", [(y * Z + z, y * Z + (z + step) % Z) for y in range(2) for z in range(Z)])


def swap_y_hi(a, flip_lo):
    pairs = []
    for gx in range(2 * Z):
        for gy in range(4 * X):
            other = (gx + Z) % (2 * Z) if flip_lo else gx
            pairs.append((gx * 4 * X + gy, other * 4 * X + (gy + 2 * X) % (4 * X)))
    return lax.ppermute(a, ("gx", "gy"), pairs)


def slot_pairs(slot):
    pairs = []
    for gx in range(2 * Z):
        for h in range(2):
            for x in range(X):
                for c in range(2):
                    first = gx * 4 * X + h * 2 * X + c
                    pairs.append((first + (x + gx + slot) % X * 2, first + x * 2))
    return pairs


def fetch(a, slot):
    return lax.ppermute(a, ("gx", "gy"), slot_pairs(slot))


def give_back(a, slot):
    return lax.ppermute(a, ("gx", "gy"), [(user, owner) for owner, user in slot_pairs(slot)])


def together(*arrays):
    return lax.optimization_barrier(arrays)


def add(*terms):
    total = terms[0].astype(F32)
    for t in terms[1:]:
        total = total + t.astype(F32)
    return total


def along_y(own):
    near, far, across = swap_y(own), swap_y_hi(own, False), swap_y_hi(own, True)
    here = jnp.concatenate([own, near], axis=1)
    there = jnp.concatenate([far, across], axis=1)
    return jnp.concatenate([here, there])


def fetch_pair(chip, pair):
    return [fetch(chip, slot) for slot in pair]


def both_cores(got):
    own = jnp.concatenate(got)
    return jnp.concatenate([own, swap_core(own)])


def quarters(product):
    n = product.shape[0] // 4
    return [jnp.concatenate([product[i * n:(i + 1) * n], product[(i + 2) * n:(i + 3) * n]]) for i in range(2)]


def as_pair(a, b):
    n = a.shape[0] // 2
    return jnp.concatenate([a[:n], b[:n], a[n:], b[n:]])


def local_step(pre, act_grad):
    cdf = 0.5 * (1.0 + jax.scipy.special.erf(pre / math.sqrt(2.0)))
    act = (pre * cdf).astype(BF16)
    slope = cdf + pre * jnp.exp(-0.5 * pre * pre) / math.sqrt(2.0 * math.pi)
    pre_grad = (act_grad * slope).astype(BF16)
    return (pre_grad, act)


def gather_z(own):
    half = own.shape[0] // 2
    behind, ahead = to_z(own, 1), to_z(own, -1)
    return behind, ahead, half


def finish_z(own, near):
    behind, ahead, half = near
    far = jnp.concatenate([to_z(behind[:half], 1), to_z(ahead[half:], -1)])
    return [own, ahead, far, behind]


def dot(a, b, da, db):
    return lax.dot_general(a, b, (((da,), (db,)), ((), ())), preferred_element_type=F32)


def shards(tokens, up_weight, down_weight, out_grad):
    y = lax.axis_index("gx") // Z
    rows, width = tokens.shape
    half = up_weight.shape[1] // 2

    def mine(w, axis):
        return lax.dynamic_slice_in_dim(w, y * half, half, axis=axis)

    def other(w, axis):
        return lax.dynamic_slice_in_dim(w, (1 - y) * half, half, axis=axis)

    def whole(own, got, axis):
        return jnp.where(y == 0, jnp.concatenate([own, got], axis=axis), jnp.concatenate([got, own], axis=axis))

    g_chip = along_y(out_grad)
    x_wide = jnp.concatenate([tokens, swap_y(tokens)], axis=1)
    down_got = swap_y(other(down_weight, 0))
    g_chip, x_wide = together(g_chip, x_wide)
    near_g = fetch_pair(g_chip, NEAR)
    g_chip, near_g, x_wide, down_got = together(g_chip, near_g, x_wide, down_got)
    far_g = fetch_pair(g_chip, FAR)
    x_chip = jnp.concatenate([x_wide, swap_y_hi(x_wide, False)])
    near_g = both_cores(near_g)
    x_chip, up_other = together(x_chip, other(up_weight, 1))
    up_got = swap_y(up_other)
    down = jnp.concatenate([mine(down_weight, 0), down_got], axis=1)
    one, three = quarters(dot(near_g, down, 1, 1).astype(BF16))
    x_chip, far_g, one, three = together(x_chip, far_g, one, three)
    one, three = to_z(one, 1), to_z(three, 3)
    far_g = both_cores(far_g)
    own, two = quarters(dot(far_g, down, 1, 1).astype(BF16))
    far_x = fetch_pair(x_chip, FAR)
    x_chip, up_got, far_x, one, three, two = together(x_chip, up_got, far_x, one, three, two)
    near_x = fetch_pair(x_chip, NEAR)
    act_grad = [own, one, three]
    two = to_z(two, 2)
    up = jnp.concatenate([mine(up_weight, 1), up_got], axis=0)

    far_x = both_cores(far_x)
    own, far = quarters(dot(far_x, up, 1, 0).astype(BF16))
    n = far.shape[0] // 2
    up_far, down_far = to_z(far[:n], 1), to_z(far[n:], 3)
    near_x, two, own = together(near_x, two, own)
    act_grad.append(two)
    near_x = both_cores(near_x)
    one, three = quarters(dot(near_x, up, 1, 0).astype(BF16))
    one = jnp.concatenate([add(one[:n], up_far).astype(BF16), one[n:]])
    three = jnp.concatenate([three[:n], add(three[n:], down_far).astype(BF16)])
    pre = [own, to_z(one, 1), to_z(three, 3)]
    pre_grad, act = local_step(add(*pre), add(*act_grad))

    def rows_back(part):
        part = dot(part, up, 1, 1).astype(BF16)
        n = part.shape[0] // 2
        return part[:n], part[n:]

    def send_back(part, others):
        return add(part, swap_core(others)).astype(BF16)

    own_back = send_back(*rows_back(pre_grad))
    behind, ahead, half = gather_z(pre_grad)
    rows_one, rows_three = rows_back(ahead), rows_back(behind)
    act, own_back, rows_one, rows_three = together(act, own_back, rows_one, rows_three)
    pre_grad = finish_z(pre_grad, (behind, ahead, half))
    act = finish_z(act, gather_z(act))
    back = [give_back(own_back, 0), give_back(send_back(*rows_one), 1), give_back(send_back(*rows_three), 3)]
    back.append(give_back(send_back(*rows_back(pre_grad[2])), 2))
    back = add(*back).astype(BF16)

    up_grad = dot(near_x, as_pair(pre_grad[1], pre_grad[3]), 0, 0)
    up_grad = up_grad + dot(far_x, as_pair(pre_grad[0], pre_grad[2]), 0, 0)
    down_grad = dot(as_pair(act[1], act[3]), near_g, 0, 0)
    down_grad = down_grad + dot(as_pair(act[0], act[2]), far_g, 0, 0)

    here, there = back[:rows], back[rows:]
    far, across = swap_y_hi(there[:, :width], False), swap_y_hi(there[:, width:], True)
    input_grad = add(here[:, :width], swap_y(here[:, width:]), far, across).astype(BF16)

    factor = 1.0 / math.sqrt(rows * lax.axis_size("gy"))
    up_grad = (up_grad * factor).astype(BF16)
    down_grad = (down_grad * factor).astype(BF16)
    up_grad = whole(up_grad[:width], swap_y(up_grad[width:]), 1)
    down_grad = whole(down_grad[:, :width], swap_y(down_grad[:, width:]), 0)
    return (input_grad, up_grad, down_grad)


def solution(mesh):
    in_specs = (P("gy", "gx"), P("gx", "gy"), P("gy", "gx"), P("gy", "gx"))
    out_specs = (P("gy", "gx"), P("gx", "gy"), P("gy", "gx"))
    return jax.shard_map(shards, mesh=mesh, in_specs=in_specs, out_specs=out_specs, check_vma=False)
```

```python
import math

import jax
import jax.numpy as jnp
from jax import lax
from jax.sharding import PartitionSpec as P

Z = 4
X = 4
NEAR, FAR = (1, 3), (0, 2)
BF16, F32 = jnp.bfloat16, jnp.float32


def swap_y(a):
    return lax.ppermute(a, "gx", [(i, (i + Z) % (2 * Z)) for i in range(2 * Z)])


def swap_core(a):
    return lax.ppermute(a, "gy", [(i, i ^ 1) for i in range(4 * X)])


def to_z(a, step):
    return lax.ppermute(a, "gx", [(y * Z + z, y * Z + (z + step) % Z) for y in range(2) for z in range(Z)])


def swap_y_hi(a, flip_lo):
    pairs = []
    for gx in range(2 * Z):
        for gy in range(4 * X):
            other = (gx + Z) % (2 * Z) if flip_lo else gx
            pairs.append((gx * 4 * X + gy, other * 4 * X + (gy + 2 * X) % (4 * X)))
    return lax.ppermute(a, ("gx", "gy"), pairs)


def slot_pairs(slot):
    pairs = []
    for gx in range(2 * Z):
        for h in range(2):
            for x in range(X):
                for c in range(2):
                    first = gx * 4 * X + h * 2 * X + c
                    pairs.append((first + (x + gx + slot) % X * 2, first + x * 2))
    return pairs


def fetch(a, slot):
    return lax.ppermute(a, ("gx", "gy"), slot_pairs(slot))


def give_back(a, slot):
    return lax.ppermute(a, ("gx", "gy"), [(user, owner) for owner, user in slot_pairs(slot)])


def together(*arrays):
    return lax.optimization_barrier(arrays)


def add(*terms):
    total = terms[0].astype(F32)
    for t in terms[1:]:
        total = total + t.astype(F32)
    return total


def along_y(own):
    near, far, across = swap_y(own), swap_y_hi(own, False), swap_y_hi(own, True)
    here = jnp.concatenate([own, near], axis=1)
    there = jnp.concatenate([far, across], axis=1)
    return jnp.concatenate([here, there])


def fetch_pair(chip, pair):
    return [fetch(chip, slot) for slot in pair]


def both_cores(got):
    own = jnp.concatenate(got)
    return jnp.concatenate([own, swap_core(own)])


def quarters(product):
    n = product.shape[0] // 4
    return [jnp.concatenate([product[i * n:(i + 1) * n], product[(i + 2) * n:(i + 3) * n]]) for i in range(2)]


def as_pair(a, b):
    n = a.shape[0] // 2
    return jnp.concatenate([a[:n], b[:n], a[n:], b[n:]])


def local_step(pre, act_grad):
    cdf = 0.5 * (1.0 + jax.scipy.special.erf(pre / math.sqrt(2.0)))
    act = (pre * cdf).astype(BF16)
    slope = cdf + pre * jnp.exp(-0.5 * pre * pre) / math.sqrt(2.0 * math.pi)
    pre_grad = (act_grad * slope).astype(BF16)
    return (pre_grad, act)


def gather_z(own):
    half = own.shape[0] // 2
    behind, ahead = to_z(own, 1), to_z(own, -1)
    return behind, ahead, half


def finish_z(own, near):
    behind, ahead, half = near
    far = jnp.concatenate([to_z(behind[:half], 1), to_z(ahead[half:], -1)])
    return [own, ahead, far, behind]


def dot(a, b, da, db):
    return lax.dot_general(a, b, (((da,), (db,)), ((), ())), preferred_element_type=F32)


def shards(tokens, up_weight, down_weight, out_grad):
    y = lax.axis_index("gx") // Z
    rows, width = tokens.shape
    half = up_weight.shape[1] // 2

    def mine(w, axis):
        return lax.dynamic_slice_in_dim(w, y * half, half, axis=axis)

    def other(w, axis):
        return lax.dynamic_slice_in_dim(w, (1 - y) * half, half, axis=axis)

    def whole(own, got, axis):
        return jnp.where(y == 0, jnp.concatenate([own, got], axis=axis), jnp.concatenate([got, own], axis=axis))

    g_chip = along_y(out_grad)
    x_wide = jnp.concatenate([tokens, swap_y(tokens)], axis=1)
    down_got = swap_y(other(down_weight, 0))
    g_chip, x_wide = together(g_chip, x_wide)
    near_g = fetch_pair(g_chip, NEAR)
    g_chip, near_g, x_wide, down_got = together(g_chip, near_g, x_wide, down_got)
    far_g = fetch_pair(g_chip, FAR)
    x_chip = jnp.concatenate([x_wide, swap_y_hi(x_wide, False)])
    near_g = both_cores(near_g)
    x_chip, up_other = together(x_chip, other(up_weight, 1))
    up_got = swap_y(up_other)
    down = jnp.concatenate([mine(down_weight, 0), down_got], axis=1)
    one, three = quarters(dot(near_g, down, 1, 1).astype(BF16))
    x_chip, far_g, one, three = together(x_chip, far_g, one, three)
    one, three = to_z(one, 1), to_z(three, 3)
    far_g = both_cores(far_g)
    own, two = quarters(dot(far_g, down, 1, 1).astype(BF16))
    far_x = fetch_pair(x_chip, FAR)
    x_chip, up_got, far_x, one, three, two = together(x_chip, up_got, far_x, one, three, two)
    near_x = fetch_pair(x_chip, NEAR)
    act_grad = [own, one, three]
    two = to_z(two, 2)
    up = jnp.concatenate([mine(up_weight, 1), up_got], axis=0)

    far_x = both_cores(far_x)
    own, far = quarters(dot(far_x, up, 1, 0).astype(BF16))
    n = far.shape[0] // 2
    up_far, down_far = to_z(far[:n], 1), to_z(far[n:], 3)
    near_x, two, own = together(near_x, two, own)
    act_grad.append(two)
    near_x = both_cores(near_x)
    one, three = quarters(dot(near_x, up, 1, 0).astype(BF16))
    one = jnp.concatenate([add(one[:n], up_far).astype(BF16), one[n:]])
    three = jnp.concatenate([three[:n], add(three[n:], down_far).astype(BF16)])
    pre = [own, to_z(one, 1), to_z(three, 3)]
    pre_grad, act = local_step(add(*pre), add(*act_grad))

    def rows_back(part):
        part = dot(part, up, 1, 1).astype(BF16)
        n = part.shape[0] // 2
        return part[:n], part[n:]

    def send_back(part, others):
        return add(part, swap_core(others)).astype(BF16)

    own_back = send_back(*rows_back(pre_grad))
    behind, ahead, half = gather_z(pre_grad)
    rows_one, rows_three = rows_back(ahead), rows_back(behind)
    act, own_back, rows_one, rows_three = together(act, own_back, rows_one, rows_three)
    pre_grad = finish_z(pre_grad, (behind, ahead, half))
    act = finish_z(act, gather_z(act))
    near_down = dot(as_pair(act[1], act[3]), near_g, 0, 0)
    near_down, act[2] = together(near_down, act[2])
    far_back = send_back(*rows_back(pre_grad[2]))
    own_back, far_back = together(own_back, far_back)
    back = [give_back(send_back(*rows_one), 1), give_back(send_back(*rows_three), 3)]
    back += [give_back(own_back, 0), give_back(far_back, 2)]
    back = add(*back).astype(BF16)

    up_grad = dot(near_x, as_pair(pre_grad[1], pre_grad[3]), 0, 0)
    up_grad = up_grad + dot(far_x, as_pair(pre_grad[0], pre_grad[2]), 0, 0)
    down_grad = near_down + dot(as_pair(act[0], act[2]), far_g, 0, 0)

    here, there = back[:rows], back[rows:]
    far, across = swap_y_hi(there[:, :width], False), swap_y_hi(there[:, width:], True)
    input_grad = add(here[:, :width], swap_y(here[:, width:]), far, across).astype(BF16)

    factor = 1.0 / math.sqrt(rows * lax.axis_size("gy"))
    up_grad = (up_grad * factor).astype(BF16)
    down_grad = (down_grad * factor).astype(BF16)
    up_got, down_other = together(swap_y(up_grad[width:]), down_grad[:, width:])
    up_grad = whole(up_grad[:width], up_got, 1)
    down_grad = whole(down_grad[:, :width], swap_y(down_other), 0)
    return (input_grad, up_grad, down_grad)


def solution(mesh):
    in_specs = (P("gy", "gx"), P("gx", "gy"), P("gy", "gx"), P("gy", "gx"))
    out_specs = (P("gy", "gx"), P("gx", "gy"), P("gy", "gx"))
    return jax.shard_map(shards, mesh=mesh, in_specs=in_specs, out_specs=out_specs, check_vma=False)
```
